128 devices in a mesh: dp: 8 (over z, core), ctx: 16 (over y, x).
Axes of the slice: x: 4, y: 4, z: 4, core: 2. Of those that a mesh axis runs over, the one named last changes fastest.
Arguments:
- attn_in: bfloat16 [8, 2048, 4096], P('dp', 'ctx'), may hold values from -6 to 6
- attn_mix: bfloat16 [8, 2048, 4096], P('dp', 'ctx'), may hold values from -6 to 6
- mlp_in: bfloat16 [8, 2048, 4096], P('dp', 'ctx'), may hold values from -6 to 6
- mlp_act: bfloat16 [8, 2048, 14336], P('dp', 'ctx'), may hold values from -6 to 6
- grad_query: bfloat16 [8, 2048, 4096], P('dp', 'ctx'), may hold values from -0.19921875 to 0.19921875
- grad_key: bfloat16 [8, 2048, 1024], P('dp', 'ctx'), may hold values from -0.19921875 to 0.19921875
- grad_value: bfloat16 [8, 2048, 1024], P('dp', 'ctx'), may hold values from -0.19921875 to 0.19921875
- grad_output: bfloat16 [8, 2048, 4096], P('dp', 'ctx'), may hold values from -0.19921875 to 0.19921875
- grad_gate: bfloat16 [8, 2048, 14336], P('dp', 'ctx'), may hold values from -0.19921875 to 0.19921875
- grad_up: bfloat16 [8, 2048, 14336], P('dp', 'ctx'), may hold values from -0.19921875 to 0.19921875
- grad_down: bfloat16 [8, 2048, 4096], P('dp', 'ctx'), may hold values from -0.19921875 to 0.19921875
- proj_attn: bfloat16 [4096, 64], replicated, may hold values from -0.09375 to 0.09375
- proj_mix: bfloat16 [4096, 64], replicated, may hold values from -0.09375 to 0.09375
- proj_mlp: bfloat16 [4096, 64], replicated, may hold values from -0.09375 to 0.09375
- proj_act: bfloat16 [14336, 64], replicated, may hold values from -0.046875 to 0.046875
- proj_query: bfloat16 [4096, 64], replicated, may hold values from -0.09375 to 0.09375
- proj_key: bfloat16 [1024, 64], replicated, may hold values from -0.1875 to 0.1875
- proj_value: bfloat16 [1024, 64], replicated, may hold values from -0.1875 to 0.1875
- proj_output: bfloat16 [4096, 64], replicated, may hold values from -0.09375 to 0.09375
- proj_gate: bfloat16 [14336, 64], replicated, may hold values from -0.046875 to 0.046875
- proj_upward: bfloat16 [14336, 64], replicated, may hold values from -0.046875 to 0.046875
- proj_down: bfloat16 [4096, 64], replicated, may hold values from -0.09375 to 0.09375
- seq_counts: int32 [8], P('dp'), may hold values from 128 to 2048, as said below
- example_ids: int32 [8], replicated, may hold values from 0 to 7, each once
Outputs:
- store: float32 [8, 7, 4096], P('dp', None, 'ctx')
The draws below stay inside these ranges and needn't reach their ends.
Inputs may be any that keep to these rules, and one draw needn't show every extreme that they name: `seq_counts`: every count is a multiple of 128; some sequence has all 2048 tokens. `example_ids`: a permutation: every store row receives exactly one sequence.
All inputs are finite; a program needn't handle non-finite values.
Results may differ from the reference program's by a relative error of at most 0.004.
Values sent between devices are 32-bit elements; how exact they have to be, the bound alone decides.
No kernel may reach another device: no remote copies, remote signals or barrier semaphores. Data moves between devices by JAX's collectives and lax.ppermute only.
A program may use at most 128 MiB of HBM per device.

```python
import jax
import jax.numpy as jnp

D = 4096
KV = 1024
FF = 14336
RANK = 64
BLOCK = 128
SEQLEN = 2048
SEQS = 8


def draw_seq_counts(key, part):
    first_key, second_key = jax.random.split(jax.random.fold_in(key, 17))
    blocks = jax.random.randint(first_key, (SEQS,), 1, SEQLEN // BLOCK + 1)
    longest = jax.random.randint(second_key, (), 0, SEQS)
    blocks = jnp.where(jnp.arange(SEQS) == longest, SEQLEN // BLOCK, blocks)
    return (blocks * BLOCK).astype(jnp.int32)


def block_scale(key, shape, shards, smallest, high):
    def one(axis_at, shards_of):
        heights = jax.random.uniform(jax.random.fold_in(jax.random.fold_in(key, 6), axis_at), (shards_of,), jnp.float32, smallest / len(shards), high / len(shards))
        return jnp.repeat(jnp.exp(heights), shape[axis_at] // shards_of).reshape((-1,) + (1,) * (len(shape) - axis_at - 1))

    gain = one(*shards[0])
    for cut in shards[1:]:
        gain = gain * one(*cut)
    return gain


def noise(rng, extent, spread, bound, shards=(), kind=jnp.bfloat16):
    drawn = jax.random.normal(rng, extent, jnp.float32) * spread
    if len(shards) > 0:
        drawn = block_scale(rng, extent, shards, -0.22, 0.18) * drawn
    return jnp.clip(drawn, min=-bound, max=bound).astype(kind)


def setup_inputs(seed: int = 0) -> dict:
    key_list = jax.random.split(jax.random.key(seed), 25)
    return {
        "attn_in": noise(key_list[0], (SEQS, SEQLEN, D), 1.0, 6.0, ((0, 8), (1, 16))),
        "attn_mix": noise(key_list[1], (SEQS, SEQLEN, D), 1.0, 6.0, ((0, 8), (1, 16))),
        "mlp_in": noise(key_list[2], (SEQS, SEQLEN, D), 1.0, 6.0, ((0, 8), (1, 16))),
        "mlp_act": noise(key_list[3], (SEQS, SEQLEN, FF), 1.0, 6.0, ((0, 8), (1, 16))),
        "grad_query": noise(key_list[4], (SEQS, SEQLEN, D), 0.03, 0.19921875, ((0, 8), (1, 16))),
        "grad_key": noise(key_list[5], (SEQS, SEQLEN, KV), 0.03, 0.19921875, ((0, 8), (1, 16))),
        "grad_value": noise(key_list[6], (SEQS, SEQLEN, KV), 0.03, 0.19921875, ((0, 8), (1, 16))),
        "grad_output": noise(key_list[7], (SEQS, SEQLEN, D), 0.03, 0.19921875, ((0, 8), (1, 16))),
        "grad_gate": noise(key_list[8], (SEQS, SEQLEN, FF), 0.03, 0.19921875, ((0, 8), (1, 16))),
        "grad_up": noise(key_list[9], (SEQS, SEQLEN, FF), 0.03, 0.19921875, ((0, 8), (1, 16))),
        "grad_down": noise(key_list[10], (SEQS, SEQLEN, D), 0.03, 0.19921875, ((0, 8), (1, 16))),
        "proj_attn": noise(key_list[11], (D, RANK), D ** -0.5, 0.09375),
        "proj_mix": noise(key_list[12], (D, RANK), D ** -0.5, 0.09375),
        "proj_mlp": noise(key_list[13], (D, RANK), D ** -0.5, 0.09375),
        "proj_act": noise(key_list[14], (FF, RANK), FF ** -0.5, 0.046875),
        "proj_query": noise(key_list[15], (D, RANK), D ** -0.5, 0.09375),
        "proj_key": noise(key_list[16], (KV, RANK), KV ** -0.5, 0.1875),
        "proj_value": noise(key_list[17], (KV, RANK), KV ** -0.5, 0.1875),
        "proj_output": noise(key_list[18], (D, RANK), D ** -0.5, 0.09375),
        "proj_gate": noise(key_list[19], (FF, RANK), FF ** -0.5, 0.046875),
        "proj_upward": noise(key_list[20], (FF, RANK), FF ** -0.5, 0.046875),
        "proj_down": noise(key_list[21], (D, RANK), D ** -0.5, 0.09375),
        "seq_counts": draw_seq_counts(jax.random.fold_in(key_list[24], 71), 0),
        "example_ids": jax.random.permutation(key_list[23], SEQS).astype(jnp.int32),
    }


def project_all(acts, projection):
    flat = acts.reshape(-1, acts.shape[-1])
    result = jnp.dot(flat, projection, preferred_element_type=jnp.float32)
    return result.astype(jnp.bfloat16).reshape(SEQS, SEQLEN, RANK)


def sketch_one(grads_proj, inputs_proj):
    return jnp.einsum('bta,btc->bac', grads_proj.astype(jnp.float32), inputs_proj.astype(jnp.float32)).reshape(SEQS, RANK * RANK)


def reference(attn_in, attn_mix, mlp_in, mlp_act, grad_query, grad_key, grad_value, grad_output, grad_gate, grad_up, grad_down, proj_attn, proj_mix, proj_mlp, proj_act, proj_query, proj_key, proj_value, proj_output, proj_gate, proj_upward, proj_down, seq_counts, example_ids):
    positions = jnp.arange(SEQLEN, dtype=jnp.int32)
    live = (positions[None, :] < seq_counts[:, None]).astype(jnp.bfloat16)[:, :, None]
    attn_p = project_all(attn_in, proj_attn)
    mix_p = project_all(attn_mix, proj_mix)
    mlp_p = project_all(mlp_in, proj_mlp)
    act_p = project_all(mlp_act, proj_act)
    pairs = [(grad_query, proj_query, attn_p), (grad_key, proj_key, attn_p), (grad_value, proj_value, attn_p), (grad_output, proj_output, mix_p), (grad_gate, proj_gate, mlp_p), (grad_up, proj_upward, mlp_p), (grad_down, proj_down, act_p)]
    sketches = []
    for grads, projection, inputs_proj in pairs:
        grads_proj = project_all(grads, projection) * live
        sketches.append(sketch_one(grads_proj, inputs_proj))
    stacked = jnp.stack(sketches, axis=1)
    return jnp.zeros_like(stacked).at[example_ids].set(stacked)
```

```python
import functools

import jax
import jax.numpy as jnp
from jax import lax
from jax.experimental import pallas as pl
from jax.experimental.pallas import tpu as pltpu
from jax.sharding import PartitionSpec as P

RANK = 64
PIECES = 16
CHUNK = 2048
GROUPS = (
    ("attn_in", ("grad_query", "grad_key", "grad_value")),
    ("attn_mix", ("grad_output",)),
    ("mlp_in", ("grad_gate", "grad_up")),
    ("mlp_act", ("grad_down",)),
)
PROJ = {
    "attn_in": "proj_attn",
    "attn_mix": "proj_mix",
    "mlp_in": "proj_mlp",
    "mlp_act": "proj_act",
    "grad_query": "proj_query",
    "grad_key": "proj_key",
    "grad_value": "proj_value",
    "grad_output": "proj_output",
    "grad_gate": "proj_gate",
    "grad_up": "proj_upward",
    "grad_down": "proj_down",
}
MAPS = ("grad_query", "grad_key", "grad_value", "grad_output", "grad_gate", "grad_up", "grad_down")
ORDER = tuple(name for first, rest in GROUPS for name in (first, *rest))
NAMES = (
    "attn_in", "attn_mix", "mlp_in", "mlp_act",
    "grad_query", "grad_key", "grad_value", "grad_output", "grad_gate", "grad_up", "grad_down",
    "proj_attn", "proj_mix", "proj_mlp", "proj_act",
    "proj_query", "proj_key", "proj_value", "proj_output", "proj_gate", "proj_upward", "proj_down",
    "seq_counts", "example_ids",
)


def sketch_kernel(widths, *refs):
    n = len(ORDER)
    counts = refs[0]
    acts = dict(zip(ORDER, refs[1 : 1 + n]))
    projs = dict(zip(ORDER, refs[1 + n : 1 + 2 * n]))
    out = refs[1 + 2 * n]
    act_bufs = dict(zip(ORDER, refs[2 + 2 * n : 2 + 3 * n]))
    proj_bufs = dict(zip(ORDER, refs[2 + 3 * n : 2 + 4 * n]))
    square, act_sem, proj_sem = refs[2 + 4 * n :]
    rows = act_bufs[ORDER[0]].shape[0]

    copies = {}
    slot = 0
    for name in ORDER:
        for start in range(0, widths[name], CHUNK):
            part = pl.ds(start, min(CHUNK, widths[name] - start))
            copies[name, start] = (
                pltpu.make_async_copy(
                    projs[name].at[:, part], proj_bufs[name].at[:, part], proj_sem.at[slot]
                ),
                pltpu.make_async_copy(
                    acts[name].at[0, :, part], act_bufs[name].at[:, part], act_sem.at[slot]
                ),
            )
            for copy in copies[name, start]:
                copy.start()
            slot += 1

    def project(name):
        total = None
        for start in range(0, widths[name], CHUNK):
            part = pl.ds(start, min(CHUNK, widths[name] - start))
            for copy in copies[name, start]:
                copy.wait()
            product = lax.dot_general(
                act_bufs[name][:, part],
                proj_bufs[name][:, part],
                (((1,), (1,)), ((), ())),
                preferred_element_type=jnp.float32,
            )
            total = product if total is None else total + product
        return total

    first_pos = lax.axis_index("ctx") * rows
    position = first_pos + lax.broadcasted_iota(jnp.int32, (rows, RANK), 0)
    live = position < counts[0]
    for first, rest in GROUPS:
        inputs_proj = project(first).astype(jnp.bfloat16)
        for name in rest:
            at = MAPS.index(name)
            grads_proj = jnp.where(live, project(name), 0.0).astype(jnp.bfloat16)
            square[at] = lax.dot_general(
                grads_proj,
                inputs_proj,
                (((0,), (0,)), ((), ())),
                preferred_element_type=jnp.float32,
            )
            step = RANK // PIECES
            lanes = [square[at, pl.ds(k, PIECES, stride=step), :] for k in range(step)]
            out[:, at, :] = jnp.concatenate(lanes, axis=1)


def sketches(values):
    widths = {name: values[name].shape[2] for name in ORDER}
    rows = values["attn_in"].shape[1]
    slots = sum(-(-width // CHUNK) for width in widths.values())
    hbm = pl.BlockSpec(memory_space=pl.ANY)
    total = sum(widths.values())
    return pl.pallas_call(
        functools.partial(sketch_kernel, widths),
        out_shape=jax.ShapeDtypeStruct((PIECES, len(MAPS), RANK * RANK // PIECES), jnp.float32),
        in_specs=[pl.BlockSpec(memory_space=pltpu.SMEM)] + [hbm] * (2 * len(ORDER)),
        out_specs=pl.BlockSpec(memory_space=pltpu.VMEM),
        scratch_shapes=[
            *[pltpu.VMEM((rows, widths[name]), jnp.bfloat16) for name in ORDER],
            *[pltpu.VMEM((RANK, widths[name]), jnp.bfloat16) for name in ORDER],
            pltpu.VMEM((len(MAPS), RANK, RANK), jnp.float32),
            pltpu.SemaphoreType.DMA((slots,)),
            pltpu.SemaphoreType.DMA((slots,)),
        ],
        compiler_params=pltpu.CompilerParams(vmem_limit_bytes=60 * 1024 * 1024),
        cost_estimate=pl.CostEstimate(
            flops=2 * rows * RANK * total, bytes_accessed=2 * (rows + RANK) * total, transcendentals=0
        ),
    )(
        values["seq_counts"],
        *[values[name] for name in ORDER],
        *[values[PROJ[name]].T for name in ORDER],
    )


def shards(*args):
    values = dict(zip(NAMES, args))
    pieces = sketches(values)
    pieces = lax.all_to_all(pieces, "ctx", 0, 0, tiled=True)
    own = jnp.sum(pieces, axis=0)
    groups = lax.axis_size("dp")
    target = values["example_ids"][lax.axis_index("dp")]
    chosen = jnp.arange(groups, dtype=jnp.int32) == target
    spread = jnp.where(chosen[:, None, None], own[None], 0.0)
    arrived = lax.all_to_all(spread, "dp", 0, 0, tiled=True)
    return jnp.sum(arrived, axis=0, keepdims=True)


def solution(mesh):
    split = P("dp", "ctx", None)
    return jax.shard_map(
        shards,
        mesh=mesh,
        in_specs=(*[split] * 11, *[P()] * 11, P("dp"), P()),
        out_specs=P("dp", None, "ctx"),
        check_vma=False,
    )
```

```python
import functools

import jax
import jax.numpy as jnp
from jax import lax
from jax.experimental import pallas as pl
from jax.experimental.pallas import tpu as pltpu
from jax.sharding import PartitionSpec as P

RANK = 64
PIECES = 16
CHUNK = 2048
GROUPS = (
    ("attn_in", ("grad_query", "grad_key", "grad_value")),
    ("attn_mix", ("grad_output",)),
    ("mlp_in", ("grad_gate", "grad_up")),
    ("mlp_act", ("grad_down",)),
)
PROJ = {
    "attn_in": "proj_attn",
    "attn_mix": "proj_mix",
    "mlp_in": "proj_mlp",
    "mlp_act": "proj_act",
    "grad_query": "proj_query",
    "grad_key": "proj_key",
    "grad_value": "proj_value",
    "grad_output": "proj_output",
    "grad_gate": "proj_gate",
    "grad_up": "proj_upward",
    "grad_down": "proj_down",
}
MAPS = ("grad_query", "grad_key", "grad_value", "grad_output", "grad_gate", "grad_up", "grad_down")
ORDER = tuple(name for first, rest in GROUPS for name in (first, *rest))
NAMES = (
    "attn_in", "attn_mix", "mlp_in", "mlp_act",
    "grad_query", "grad_key", "grad_value", "grad_output", "grad_gate", "grad_up", "grad_down",
    "proj_attn", "proj_mix", "proj_mlp", "proj_act",
    "proj_query", "proj_key", "proj_value", "proj_output", "proj_gate", "proj_upward", "proj_down",
    "seq_counts", "example_ids",
)


SLABS = 4


def sketch_kernel(widths, *refs):
    n = len(ORDER)
    counts = refs[0]
    acts = dict(zip(ORDER, refs[1 : 1 + n]))
    projs = dict(zip(ORDER, refs[1 + n : 1 + 2 * n]))
    out = refs[1 + 2 * n]
    act_bufs = dict(zip(ORDER, refs[2 + 2 * n : 2 + 3 * n]))
    proj_bufs = dict(zip(ORDER, refs[2 + 3 * n : 2 + 4 * n]))
    square, act_sem, proj_sem = refs[2 + 4 * n :]
    rows = acts[ORDER[0]].shape[1]

    copies = {}
    for at, name in enumerate(ORDER):
        slab = widths[name] // SLABS
        copies[name] = []
        for k in range(SLABS):
            part = pl.ds(k * slab, slab)
            copies[name] += [
                pltpu.make_async_copy(
                    projs[name].at[:, part],
                    proj_bufs[name].at[pl.ds(k * RANK, RANK), :],
                    proj_sem.at[at * SLABS + k],
                ),
                pltpu.make_async_copy(
                    acts[name].at[0, :, part],
                    act_bufs[name].at[pl.ds(k * rows, rows), :],
                    act_sem.at[at * SLABS + k],
                ),
            ]
        for copy in copies[name]:
            copy.start()

    def project(name):
        for copy in copies[name]:
            copy.wait()
        product = lax.dot_general(
            proj_bufs[name][...],
            act_bufs[name][...],
            (((1,), (1,)), ((), ())),
            preferred_element_type=jnp.float32,
        )
        blocks = [
            product[k * RANK : (k + 1) * RANK, k * rows : (k + 1) * rows] for k in range(SLABS)
        ]
        return functools.reduce(lambda a, b: a + b, blocks)

    first_pos = lax.axis_index("ctx") * rows
    position = first_pos + lax.broadcasted_iota(jnp.int32, (RANK, rows), 1)
    live = position < counts[0]
    for first, rest in GROUPS:
        inputs_proj = project(first).astype(jnp.bfloat16)
        for name in rest:
            at = MAPS.index(name)
            grads_proj = jnp.where(live, project(name), 0.0).astype(jnp.bfloat16)
            square[at] = lax.dot_general(
                grads_proj,
                inputs_proj,
                (((1,), (1,)), ((), ())),
                preferred_element_type=jnp.float32,
            )
            step = RANK // PIECES
            lanes = [square[at, pl.ds(k, PIECES, stride=step), :] for k in range(step)]
            out[:, at, :] = jnp.concatenate(lanes, axis=1)


def sketches(values):
    widths = {name: values[name].shape[2] for name in ORDER}
    rows = values["attn_in"].shape[1]
    hbm = pl.BlockSpec(memory_space=pl.ANY)
    total = sum(widths.values())
    return pl.pallas_call(
        functools.partial(sketch_kernel, widths),
        out_shape=jax.ShapeDtypeStruct((PIECES, len(MAPS), RANK * RANK // PIECES), jnp.float32),
        in_specs=[pl.BlockSpec(memory_space=pltpu.SMEM)] + [hbm] * (2 * len(ORDER)),
        out_specs=pl.BlockSpec(memory_space=pltpu.VMEM),
        scratch_shapes=[
            *[pltpu.VMEM((SLABS * rows, widths[name] // SLABS), jnp.bfloat16) for name in ORDER],
            *[pltpu.VMEM((SLABS * RANK, widths[name] // SLABS), jnp.bfloat16) for name in ORDER],
            pltpu.VMEM((len(MAPS), RANK, RANK), jnp.float32),
            pltpu.SemaphoreType.DMA((SLABS * len(ORDER),)),
            pltpu.SemaphoreType.DMA((SLABS * len(ORDER),)),
        ],
        compiler_params=pltpu.CompilerParams(vmem_limit_bytes=60 * 1024 * 1024),
        cost_estimate=pl.CostEstimate(
            flops=2 * rows * RANK * total, bytes_accessed=2 * (rows + RANK) * total, transcendentals=0
        ),
    )(
        values["seq_counts"],
        *[values[name] for name in ORDER],
        *[values[PROJ[name]].T for name in ORDER],
    )


def route_rows(own, example_ids):
    groups = lax.axis_size("dp")
    me = lax.axis_index("dp")
    slots = jnp.arange(groups, dtype=jnp.int32)
    held = jnp.bitwise_xor(me, jnp.array([0, 1, 3, 2], jnp.int32))
    rows = jnp.sum(jnp.where(held[:, None] == slots[None, :], example_ids[None, :], 0), axis=1)
    keep = (rows == me)[:, None, None]
    give = (rows == jnp.bitwise_xor(me, 7))[:, None, None]

    def swap(value, flip):
        return lax.ppermute(value, "dp", [(i, i ^ flip) for i in range(groups)])

    two = jnp.stack([own, swap(own, 1)])
    four = jnp.concatenate([two, swap(two, 3)])
    arrived = swap(jnp.sum(jnp.where(give, four, 0.0), axis=0), 7)
    return (jnp.sum(jnp.where(keep, four, 0.0), axis=0) + arrived)[None]


def shards(*args):
    values = dict(zip(NAMES, args))
    pieces = sketches(values)
    pieces = lax.all_to_all(pieces, "ctx", 0, 0, tiled=True)
    own = jnp.sum(pieces, axis=0)
    return route_rows(own, values["example_ids"])


def solution(mesh):
    split = P("dp", "ctx", None)
    return jax.shard_map(
        shards,
        mesh=mesh,
        in_specs=(*[split] * 11, *[P()] * 11, P("dp"), P()),
        out_specs=P("dp", None, "ctx"),
        check_vma=False,
    )
```

```python
import functools

import jax
import jax.numpy as jnp
from jax import lax
from jax.experimental import pallas as pl
from jax.experimental.pallas import tpu as pltpu
from jax.sharding import PartitionSpec as P

RANK = 64
PIECES = 16
GROUPS = (
    ("attn_in", ("grad_query", "grad_key", "grad_value",)),
    ("attn_mix", ("grad_output",)),
    ("mlp_in", ("grad_gate", "grad_up",)),
    ("mlp_act", ("grad_down",)),
)
PROJ = {
    "attn_in": "proj_attn",
    "attn_mix": "proj_mix",
    "mlp_in": "proj_mlp",
    "mlp_act": "proj_act",
    "grad_query": "proj_query",
    "grad_key": "proj_key",
    "grad_value": "proj_value",
    "grad_output": "proj_output",
    "grad_gate": "proj_gate",
    "grad_up": "proj_upward",
    "grad_down": "proj_down",
}
MAPS = ("grad_query", "grad_key", "grad_value", "grad_output", "grad_gate", "grad_up", "grad_down")
ORDER = tuple(name for first, rest in GROUPS for name in (first, *rest))
NAMES = (
    "attn_in", "attn_mix", "mlp_in", "mlp_act",
    "grad_query", "grad_key", "grad_value", "grad_output", "grad_gate", "grad_up", "grad_down",
    "proj_attn", "proj_mix", "proj_mlp", "proj_act",
    "proj_query", "proj_key", "proj_value", "proj_output", "proj_gate", "proj_upward", "proj_down",
    "seq_counts", "example_ids",
)


SLABS = 4


def sketch_kernel(widths, *refs):
    n = len(ORDER)
    acts = dict(zip(ORDER, refs[:n]))
    projs = dict(zip(ORDER, refs[n : 2 * n]))
    out = refs[2 * n]
    act_bufs = dict(zip(ORDER, refs[1 + 2 * n : 1 + 3 * n]))
    proj_bufs = dict(zip(ORDER, refs[1 + 3 * n : 1 + 4 * n]))
    square, act_sem, proj_sem = refs[1 + 4 * n :]
    rows = acts[ORDER[0]].shape[1]

    copies = {
        name: (
            pltpu.make_async_copy(projs[name], proj_bufs[name], proj_sem.at[k]),
            pltpu.make_async_copy(acts[name].at[0], act_bufs[name], act_sem.at[k]),
        )
        for k, name in enumerate(ORDER)
    }
    for name in ORDER:
        for copy in copies[name]:
            copy.start()

    def project(name):
        for copy in copies[name]:
            copy.wait()
        slab = widths[name] // SLABS
        parts = [pl.ds(k * slab, slab) for k in range(SLABS)]
        product = lax.dot_general(
            jnp.concatenate([proj_bufs[name][:, part] for part in parts], axis=0),
            jnp.concatenate([act_bufs[name][:, part] for part in parts], axis=0),
            (((1,), (1,)), ((), ())),
            preferred_element_type=jnp.float32,
        )
        blocks = [
            product[k * RANK : (k + 1) * RANK, k * rows : (k + 1) * rows] for k in range(SLABS)
        ]
        return functools.reduce(jnp.add, blocks).astype(jnp.bfloat16)

    for first, rest in GROUPS:
        inputs_proj = project(first)
        grads_proj = [project(name) for name in rest]
        at = MAPS.index(rest[0]) * RANK
        size = len(rest) * RANK
        square[pl.ds(at, size), :] = lax.dot_general(
            jnp.concatenate(grads_proj, axis=0),
            inputs_proj,
            (((1,), (1,)), ((), ())),
            preferred_element_type=jnp.float32,
        )
        step = RANK // PIECES
        for name in rest:
            at = MAPS.index(name)
            lanes = [square[pl.ds(at * RANK + k, PIECES, stride=step), :] for k in range(step)]
            out[:, at, :] = jnp.concatenate(lanes, axis=1)


def sketches(values):
    widths = {name: values[name].shape[2] for name in ORDER}
    rows = values["attn_in"].shape[1]
    hbm = pl.BlockSpec(memory_space=pl.ANY)
    total = sum(widths.values())
    return pl.pallas_call(
        functools.partial(sketch_kernel, widths),
        out_shape=jax.ShapeDtypeStruct((PIECES, len(MAPS), RANK * RANK // PIECES), jnp.float32),
        in_specs=[hbm] * (2 * len(ORDER)),
        out_specs=pl.BlockSpec(memory_space=pltpu.VMEM),
        scratch_shapes=[
            *[pltpu.VMEM((rows, widths[name]), jnp.bfloat16) for name in ORDER],
            *[pltpu.VMEM((RANK, widths[name]), jnp.bfloat16) for name in ORDER],
            pltpu.VMEM((len(MAPS) * RANK, RANK), jnp.float32),
            pltpu.SemaphoreType.DMA((len(ORDER),)),
            pltpu.SemaphoreType.DMA((len(ORDER),)),
        ],
        compiler_params=pltpu.CompilerParams(vmem_limit_bytes=60 * 1024 * 1024),
        cost_estimate=pl.CostEstimate(
            flops=2 * rows * RANK * total, bytes_accessed=2 * (rows + RANK) * total, transcendentals=0
        ),
    )(
        *[values[name] for name in ORDER],
        *[values[PROJ[name]].T for name in ORDER],
    )


def route_rows(own, example_ids):
    groups = lax.axis_size("dp")
    me = lax.axis_index("dp")
    slots = jnp.arange(groups, dtype=jnp.int32)
    held = jnp.bitwise_xor(me, jnp.array([0, 1, 3, 2], jnp.int32))
    rows = jnp.sum(jnp.where(held[:, None] == slots[None, :], example_ids[None, :], 0), axis=1)
    keep = (rows == me)[:, None, None]
    give = (rows == jnp.bitwise_xor(me, 7))[:, None, None]

    def swap(value, flip):
        return lax.ppermute(value, "dp", [(i, i ^ flip) for i in range(groups)])

    two = jnp.stack([own, swap(own, 1)])
    four = jnp.concatenate([two, swap(two, 3)])
    arrived = swap(jnp.sum(jnp.where(give, four, 0.0), axis=0), 7)
    return (jnp.sum(jnp.where(keep, four, 0.0), axis=0) + arrived)[None]


def shards(*args):
    values = dict(zip(NAMES, args))
    pieces = sketches(values)
    pieces = lax.all_to_all(pieces, "ctx", 0, 0, tiled=True)
    block = values["attn_in"].shape[1]
    firsts = jnp.arange(pieces.shape[0], dtype=jnp.int32) * block
    live = firsts < values["seq_counts"][0]
    own = jnp.sum(jnp.where(live[:, None, None], pieces, 0.0), axis=0)
    return route_rows(own, values["example_ids"])


def solution(mesh):
    split = P("dp", "ctx", None)
    return jax.shard_map(
        shards,
        mesh=mesh,
        in_specs=(*[split] * 11, *[P()] * 11, P("dp"), P()),
        out_specs=P("dp", None, "ctx"),
        check_vma=False,
    )
```

```python
import functools

import jax
import jax.numpy as jnp
from jax import lax
from jax.experimental import pallas as pl
from jax.experimental.pallas import tpu as pltpu
from jax.sharding import PartitionSpec as P

RANK = 64
PIECES = 16
GROUPS = (
    ("attn_in", ("grad_query", "grad_key", "grad_value",)),
    ("attn_mix", ("grad_output",)),
    ("mlp_in", ("grad_gate", "grad_up",)),
    ("mlp_act", ("grad_down",)),
)
PROJ = {
    "attn_in": "proj_attn",
    "attn_mix": "proj_mix",
    "mlp_in": "proj_mlp",
    "mlp_act": "proj_act",
    "grad_query": "proj_query",
    "grad_key": "proj_key",
    "grad_value": "proj_value",
    "grad_output": "proj_output",
    "grad_gate": "proj_gate",
    "grad_up": "proj_upward",
    "grad_down": "proj_down",
}
MAPS = ("grad_query", "grad_key", "grad_value", "grad_output", "grad_gate", "grad_up", "grad_down")
ORDER = tuple(name for first, rest in GROUPS for name in (first, *rest))
NAMES = (
    "attn_in", "attn_mix", "mlp_in", "mlp_act",
    "grad_query", "grad_key", "grad_value", "grad_output", "grad_gate", "grad_up", "grad_down",
    "proj_attn", "proj_mix", "proj_mlp", "proj_act",
    "proj_query", "proj_key", "proj_value", "proj_output", "proj_gate", "proj_upward", "proj_down",
    "seq_counts", "example_ids",
)

SLABS = 4
PART = 7168


def sketch_kernel(widths, *refs):
    n = len(ORDER)
    acts = dict(zip(ORDER, refs[:n]))
    projs = dict(zip(ORDER, refs[n : 2 * n]))
    out = refs[2 * n]
    act_bufs = dict(zip(ORDER, refs[1 + 2 * n : 1 + 3 * n]))
    proj_bufs = dict(zip(ORDER, refs[1 + 3 * n : 1 + 4 * n]))
    square, act_sem, proj_sem = refs[1 + 4 * n :]
    rows = acts[ORDER[0]].shape[1]

    copies = {}
    slot = 0
    for name in ORDER:
        copies[name] = []
        for start in range(0, widths[name], PART):
            part = pl.ds(start, min(PART, widths[name] - start))
            pair = (
                pltpu.make_async_copy(
                    projs[name].at[:, part], proj_bufs[name].at[:, part], proj_sem.at[slot]
                ),
                pltpu.make_async_copy(
                    acts[name].at[0, :, part], act_bufs[name].at[:, part], act_sem.at[slot]
                ),
            )
            for copy in pair:
                copy.start()
            copies[name].append((start, part.size, pair))
            slot += 1

    def project(name):
        total = None
        for start, width, pair in copies[name]:
            for copy in pair:
                copy.wait()
            slab = width // SLABS
            slabs = [pl.ds(start + k * slab, slab) for k in range(SLABS)]
            product = lax.dot_general(
                jnp.concatenate([proj_bufs[name][:, at] for at in slabs], axis=0),
                jnp.concatenate([act_bufs[name][:, at] for at in slabs], axis=0),
                (((1,), (1,)), ((), ())),
                preferred_element_type=jnp.float32,
            )
            for k in range(SLABS):
                block = product[k * RANK : (k + 1) * RANK, k * rows : (k + 1) * rows]
                total = block if total is None else total + block
        return total.astype(jnp.bfloat16)

    for first, rest in GROUPS:
        inputs_proj = project(first)
        grads_proj = [project(name) for name in rest]
        at = MAPS.index(rest[0]) * RANK
        size = len(rest) * RANK
        square[pl.ds(at, size), :] = lax.dot_general(
            jnp.concatenate(grads_proj, axis=0),
            inputs_proj,
            (((1,), (1,)), ((), ())),
            preferred_element_type=jnp.float32,
        )
        step = RANK // PIECES
        for name in rest:
            at = MAPS.index(name)
            lanes = [square[pl.ds(at * RANK + k, PIECES, stride=step), :] for k in range(step)]
            out[:, at, :] = jnp.concatenate(lanes, axis=1)


def sketches(values):
    widths = {name: values[name].shape[2] for name in ORDER}
    rows = values["attn_in"].shape[1]
    hbm = pl.BlockSpec(memory_space=pl.ANY)
    total = sum(widths.values())
    parts = sum(-(-width // PART) for width in widths.values())
    return pl.pallas_call(
        functools.partial(sketch_kernel, widths),
        out_shape=jax.ShapeDtypeStruct((PIECES, len(MAPS), RANK * RANK // PIECES), jnp.float32),
        in_specs=[hbm] * (2 * len(ORDER)),
        out_specs=pl.BlockSpec(memory_space=pltpu.VMEM),
        scratch_shapes=[
            *[pltpu.VMEM((rows, widths[name]), jnp.bfloat16) for name in ORDER],
            *[pltpu.VMEM((RANK, widths[name]), jnp.bfloat16) for name in ORDER],
            pltpu.VMEM((len(MAPS) * RANK, RANK), jnp.float32),
            pltpu.SemaphoreType.DMA((parts,)),
            pltpu.SemaphoreType.DMA((parts,)),
        ],
        compiler_params=pltpu.CompilerParams(vmem_limit_bytes=60 * 1024 * 1024),
        cost_estimate=pl.CostEstimate(
            flops=2 * rows * RANK * total, bytes_accessed=2 * (rows + RANK) * total, transcendentals=0
        ),
    )(
        *[values[name] for name in ORDER],
        *[values[PROJ[name]].T for name in ORDER],
    )


def route_rows(own, example_ids):
    groups = lax.axis_size("dp")
    me = lax.axis_index("dp")
    slots = jnp.arange(groups, dtype=jnp.int32)
    held = jnp.bitwise_xor(me, jnp.array([0, 1, 3, 2], jnp.int32))
    rows = jnp.sum(jnp.where(held[:, None] == slots[None, :], example_ids[None, :], 0), axis=1)
    keep = (rows == me)[:, None, None]
    give = (rows == jnp.bitwise_xor(me, 5))[:, None, None]

    def swap(value, flip):
        return lax.ppermute(value, "dp", [(i, i ^ flip) for i in range(groups)])

    two = jnp.stack([own, swap(own, 1)])
    four = jnp.concatenate([two, swap(two, 3)])
    arrived = swap(jnp.sum(jnp.where(give, four, 0.0), axis=0), 5)
    return (jnp.sum(jnp.where(keep, four, 0.0), axis=0) + arrived)[None]


def shards(*args):
    values = dict(zip(NAMES, args))
    pieces = sketches(values)
    pieces = lax.all_to_all(pieces, "ctx", 0, 0, tiled=True)
    block = values["attn_in"].shape[1]
    firsts = jnp.arange(pieces.shape[0], dtype=jnp.int32) * block
    live = firsts < values["seq_counts"][0]
    own = jnp.sum(jnp.where(live[:, None, None], pieces, 0.0), axis=0)
    return route_rows(own, values["example_ids"])


def solution(mesh):
    split = P("dp", "ctx", None)
    return jax.shard_map(
        shards,
        mesh=mesh,
        in_specs=(*[split] * 11, *[P()] * 11, P("dp"), P()),
        out_specs=P("dp", None, "ctx"),
        check_vma=False,
    )
```

```python
import functools

import jax
import jax.numpy as jnp
from jax import lax
from jax.experimental import pallas as pl
from jax.experimental.pallas import tpu as pltpu
from jax.sharding import PartitionSpec as P

RANK = 64
PIECES = 16
GROUPS = (
    ("attn_in", ("grad_query", "grad_key", "grad_value",)),
    ("attn_mix", ("grad_output",)),
    ("mlp_in", ("grad_gate", "grad_up",)),
    ("mlp_act", ("grad_down",)),
)
PROJ = {
    "attn_in": "proj_attn",
    "attn_mix": "proj_mix",
    "mlp_in": "proj_mlp",
    "mlp_act": "proj_act",
    "grad_query": "proj_query",
    "grad_key": "proj_key",
    "grad_value": "proj_value",
    "grad_output": "proj_output",
    "grad_gate": "proj_gate",
    "grad_up": "proj_upward",
    "grad_down": "proj_down",
}
MAPS = ("grad_query", "grad_key", "grad_value", "grad_output", "grad_gate", "grad_up", "grad_down")
ORDER = tuple(name for first, rest in GROUPS for name in (first, *rest))
NAMES = (
    "attn_in", "attn_mix", "mlp_in", "mlp_act",
    "grad_query", "grad_key", "grad_value", "grad_output", "grad_gate", "grad_up", "grad_down",
    "proj_attn", "proj_mix", "proj_mlp", "proj_act",
    "proj_query", "proj_key", "proj_value", "proj_output", "proj_gate", "proj_upward", "proj_down",
    "seq_counts", "example_ids",
)

SLABS = 4
PART = 7168


def sketch_kernel(widths, *refs):
    n = len(ORDER)
    acts = dict(zip(ORDER, refs[:n]))
    projs = dict(zip(ORDER, refs[n : 2 * n]))
    out = refs[2 * n]
    act_bufs = dict(zip(ORDER, refs[1 + 2 * n : 1 + 3 * n]))
    proj_bufs = dict(zip(ORDER, refs[1 + 3 * n : 1 + 4 * n]))
    square, act_sem, proj_sem = refs[1 + 4 * n :]
    rows = acts[ORDER[0]].shape[1]

    copies = {}
    slot = 0
    for name in ORDER:
        copies[name] = []
        for start in range(0, widths[name], PART):
            part = pl.ds(start, min(PART, widths[name] - start))
            pair = (
                pltpu.make_async_copy(
                    projs[name].at[:, part], proj_bufs[name].at[:, part], proj_sem.at[slot]
                ),
                pltpu.make_async_copy(
                    acts[name].at[0, :, part], act_bufs[name].at[:, part], act_sem.at[slot]
                ),
            )
            for copy in pair:
                copy.start()
            copies[name].append((start, part.size, pair))
            slot += 1

    def project(name):
        total = None
        for start, width, pair in copies[name]:
            for copy in pair:
                copy.wait()
            slab = width // SLABS
            slabs = [pl.ds(start + k * slab, slab) for k in range(SLABS)]
            product = lax.dot_general(
                jnp.concatenate([proj_bufs[name][:, at] for at in slabs], axis=0),
                jnp.concatenate([act_bufs[name][:, at] for at in slabs], axis=0),
                (((1,), (1,)), ((), ())),
                preferred_element_type=jnp.float32,
            )
            for k in range(SLABS):
                block = product[k * RANK : (k + 1) * RANK, k * rows : (k + 1) * rows]
                total = block if total is None else total + block
        return total.astype(jnp.bfloat16)

    for first, rest in GROUPS:
        inputs_proj = project(first)
        grads_proj = [project(name) for name in rest]
        at = MAPS.index(rest[0]) * RANK
        size = len(rest) * RANK
        square[pl.ds(at, size), :] = lax.dot_general(
            jnp.concatenate(grads_proj, axis=0),
            inputs_proj,
            (((1,), (1,)), ((), ())),
            preferred_element_type=jnp.float32,
        )
        step = RANK // PIECES
        for name in rest:
            at = MAPS.index(name)
            lanes = [square[pl.ds(at * RANK + k, PIECES, stride=step), :] for k in range(step)]
            out[:, at, :] = jnp.concatenate(lanes, axis=1)


def sketches(values):
    widths = {name: values[name].shape[2] for name in ORDER}
    rows = values["attn_in"].shape[1]
    hbm = pl.BlockSpec(memory_space=pl.ANY)
    total = sum(widths.values())
    parts = sum(-(-width // PART) for width in widths.values())
    return pl.pallas_call(
        functools.partial(sketch_kernel, widths),
        out_shape=jax.ShapeDtypeStruct((PIECES, len(MAPS), RANK * RANK // PIECES), jnp.float32),
        in_specs=[hbm] * (2 * len(ORDER)),
        out_specs=pl.BlockSpec(memory_space=pltpu.VMEM),
        scratch_shapes=[
            *[pltpu.VMEM((rows, widths[name]), jnp.bfloat16) for name in ORDER],
            *[pltpu.VMEM((RANK, widths[name]), jnp.bfloat16) for name in ORDER],
            pltpu.VMEM((len(MAPS) * RANK, RANK), jnp.float32),
            pltpu.SemaphoreType.DMA((parts,)),
            pltpu.SemaphoreType.DMA((parts,)),
        ],
        compiler_params=pltpu.CompilerParams(vmem_limit_bytes=60 * 1024 * 1024),
        cost_estimate=pl.CostEstimate(
            flops=2 * rows * RANK * total, bytes_accessed=2 * (rows + RANK) * total, transcendentals=0
        ),
    )(
        *[values[name] for name in ORDER],
        *[values[PROJ[name]].T for name in ORDER],
    )


def route_rows(own, example_ids):
    groups = lax.axis_size("dp")
    me = lax.axis_index("dp")
    slots = jnp.arange(groups, dtype=jnp.int32)
    held = jnp.bitwise_xor(me, jnp.array([0, 1, 5, 4], jnp.int32))
    rows = jnp.sum(jnp.where(held[:, None] == slots[None, :], example_ids[None, :], 0), axis=1)
    keep = (rows == me)[:, None, None]
    give = (rows == jnp.bitwise_xor(me, 3))[:, None, None]

    def swap(value, flip):
        return lax.ppermute(value, "dp", [(i, i ^ flip) for i in range(groups)])

    two = jnp.stack([own, swap(own, 1)])
    four = jnp.concatenate([two, swap(two, 5)])
    arrived = swap(jnp.sum(jnp.where(give, four, 0.0), axis=0), 3)
    return (jnp.sum(jnp.where(keep, four, 0.0), axis=0) + arrived)[None]


def shards(*args):
    values = dict(zip(NAMES, args))
    pieces = sketches(values)
    pieces = lax.all_to_all(pieces, "ctx", 0, 0, tiled=True)
    block = values["attn_in"].shape[1]
    firsts = jnp.arange(pieces.shape[0], dtype=jnp.int32) * block
    live = firsts < values["seq_counts"][0]
    own = jnp.sum(jnp.where(live[:, None, None], pieces, 0.0), axis=0)
    return route_rows(own, values["example_ids"])


def solution(mesh):
    split = P("dp", "ctx", None)
    return jax.shard_map(
        shards,
        mesh=mesh,
        in_specs=(*[split] * 11, *[P()] * 11, P("dp"), P()),
        out_specs=P("dp", None, "ctx"),
        check_vma=False,
    )
```
